32 devices in a mesh: groups: 2 (over y), block: 4 (over x, core), tile: 4 (over z).
Axes of the slice: x: 2, y: 2, z: 4, core: 2. Of those that a mesh axis runs over, the one named last changes fastest.
Arguments:
- queries: float32 [8, 4, 16, 24, 1024], P(('groups', 'block'), 'tile'), parts along dimension 0
- keys: float32 [8, 4, 16, 24, 1024], P(('groups', 'block'), 'tile'), parts along dimension 0
- values: float32 [8, 4, 16, 24, 1024], P(('groups', 'block'), 'tile'), parts along dimension 0, may hold values from -6 to 6
- radii: int32 [4], replicated, may hold values from 1 to 4, as said below
Outputs:
- local_out: float32 [8, 4, 16, 24, 1024], P(('groups', 'block'), 'tile'), parts along dimension 0
- global_out: float32 [8, 4, 16, 24, 1024], P(('groups', 'block'), 'tile'), parts along dimension 0
The draws below stay inside these ranges and needn't reach their ends.
There are 2 independent parts, one for each index of `groups`. The reference program is written for one: setup_inputs(seed, part) draws one part's arguments, and reference() takes and returns one part's arrays. A program takes and returns all parts, laid end to end along the dimension named above; an argument that names none is the same for every part. Nothing has to cross between parts.
Inputs may be any that keep to these rules, and one draw needn't show every extreme that they name: `radii`: every head's radius is at least 1 and some head has radius 4.
All inputs are finite; a program needn't handle non-finite values.
Results may differ from the reference program's by a relative error of at most 0.0003.
Values sent between devices are 32-bit elements; how exact they have to be, the bound alone decides.
A program may use at most 128 MiB of HBM per device.

```python
import math
import jax
import jax.numpy as jnp
from jax import lax

HEADS = 4
D = 1024
TILE_ROWS = 16
TILE_COLS = 24
R_MAX = 4
TILES = 4
GRID_C = 2
GRID_R = 2
HEIGHT = 32
WIDTH = 48
FRAMES = 4


def paired(key):
    base = jax.random.fold_in(key, 7)
    shape = (FRAMES, TILES, TILE_ROWS, TILE_COLS, D)
    query_draw = jnp.clip(jax.random.normal(jax.random.fold_in(base, 1), shape, jnp.float32), -5.0, 5.0)
    key_draw = jnp.clip(jax.random.normal(jax.random.fold_in(base, 2), shape, jnp.float32), -5.0, 5.0)
    return (query_draw, key_draw)


def draw_queries(key, part):
    return paired(key)[0]


def draw_keys(key, part):
    return paired(key)[1]


def draw_radii(key, part):
    chosen = jax.random.randint(jax.random.fold_in(key, 3), (HEADS,), 1, R_MAX + 1)
    widest = jax.random.randint(jax.random.fold_in(key, 4), (), 0, HEADS)
    return chosen.at[widest].set(R_MAX).astype(jnp.int32)


def block_scale(key, dims, shards, smallest, largest):
    factor_of, own = 1.0, jax.random.fold_in(key, 6)
    for dim, shards_of in shards:
        steps = jnp.exp(jax.random.uniform(jax.random.fold_in(own, dim), (shards_of,), jnp.float32, smallest / len(shards), largest / len(shards)))
        factor_of = factor_of * jnp.repeat(steps, dims[dim] // shards_of).reshape([-1 if axis == dim else 1 for axis in range(len(dims))])
    return factor_of


def normal_values(key, shape, spread, bound, shards=(), kind=jnp.bfloat16):
    array = jax.random.normal(key, shape, jnp.float32) * spread
    if len(shards) > 0:
        array = block_scale(key, shape, shards, -0.22, 0.18) * array
    return jnp.clip(array, min=-bound, max=bound).astype(kind)


def setup_inputs(seed: int = 0, part: int = 0) -> dict:
    key_list = jax.random.split(jax.random.key(seed), 5)
    own_keys = jax.random.split(jax.random.fold_in(key_list[4], part), 5)
    queries = draw_queries(jax.random.fold_in(jax.random.fold_in(key_list[4], part), 71), part)
    keys = draw_keys(jax.random.fold_in(jax.random.fold_in(key_list[4], part), 71), part)
    values = normal_values(own_keys[2], (FRAMES, TILES, TILE_ROWS, TILE_COLS, D), 1.0, 6.0, ((0, 4), (1, 4)), jnp.float32)
    radii = draw_radii(jax.random.fold_in(key_list[4], 71), part)
    return dict(queries=queries, keys=keys, values=values, radii=radii)


def neighborhood(query_tile, key_tile, value_tile, radii, row_start, col_start, height, width):
    rows, cols, dim = query_tile.shape
    head_count = radii.shape[0]
    head_dim = dim // head_count
    key_h = key_tile.shape[0]
    key_w = key_tile.shape[1]
    row_margin = (key_h - rows) // 2
    col_margin = (key_w - cols) // 2
    query_rows = query_tile.reshape(rows * cols, head_count, head_dim)
    key_rows = key_tile.reshape(key_h * key_w, head_count, head_dim)
    value_rows = value_tile.reshape(key_h * key_w, head_count, head_dim)
    scores = jnp.einsum('qhd,khd->hqk', query_rows, key_rows, precision=lax.Precision.HIGHEST) / math.sqrt(head_dim)
    query_pos = jnp.arange(rows * cols, dtype=jnp.int32)
    key_pos = jnp.arange(key_h * key_w, dtype=jnp.int32)
    query_row = query_pos // cols
    query_col = query_pos % cols
    key_row = key_pos // key_w - row_margin
    key_col = key_pos % key_w - col_margin
    reach = jnp.maximum(jnp.abs(query_row[:, None] - key_row[None, :]), jnp.abs(query_col[:, None] - key_col[None, :]))
    inside = (col_start + key_col >= 0) & (col_start + key_col < width) & (row_start + key_row >= 0) & (row_start + key_row < height)
    allowed = (reach[None, :, :] <= radii[:, None, None]) & inside[None, None, :]
    scores = jnp.where(allowed, scores, jnp.float32(-1e+30))
    top = lax.optimization_barrier(jnp.max(scores, axis=-1, keepdims=True))
    weights = jnp.exp(scores - top)
    weights = weights / lax.optimization_barrier(jnp.sum(weights, axis=-1, keepdims=True))
    result = jnp.einsum('hqk,khd->qhd', weights, value_rows, precision=lax.Precision.HIGHEST)
    return result.reshape(rows, cols, dim)

def linear_out(query_rows, state, zsum, vsum, count):
    head_dim = state.shape[1]
    feature = jax.nn.relu(query_rows)
    numer = jnp.einsum('qhd,hde->qhe', feature, state, precision=lax.Precision.HIGHEST) / math.sqrt(head_dim) + vsum[None, :, :]
    denom = jnp.einsum('qhd,hd->qh', feature, zsum, precision=lax.Precision.HIGHEST) / math.sqrt(head_dim) + count
    return numer / denom[:, :, None]

def to_frame(tiles):
    dim = tiles.shape[-1]
    placed = jnp.roll(tiles, 1, axis=0)
    grid = placed.reshape(GRID_R, GRID_C, TILE_ROWS, TILE_COLS, dim)
    return jnp.transpose(grid, (0, 2, 1, 3, 4)).reshape(HEIGHT, WIDTH, dim)

def reference(queries, keys, values, radii):
    frames = queries.shape[0]
    dim = queries.shape[-1]
    head_count = radii.shape[0]
    head_dim = dim // head_count
    local_list = []
    global_list = []
    state = jnp.zeros((head_count, head_dim, head_dim), jnp.float32)
    zsum = jnp.zeros((head_count, head_dim), jnp.float32)
    vsum = jnp.zeros((head_count, head_dim), jnp.float32)
    for frame in range(frames):
        pad_keys = jnp.pad(to_frame(keys[frame]), ((R_MAX, R_MAX), (R_MAX, R_MAX), (0, 0)))
        pad_values = jnp.pad(to_frame(values[frame]), ((R_MAX, R_MAX), (R_MAX, R_MAX), (0, 0)))
        frame_queries = queries[frame]

        def one_tile(tile_idx):
            position = ((tile_idx + 1) % TILES).astype(jnp.int32)
            row_start = (position // GRID_C * TILE_ROWS).astype(jnp.int32)
            col_start = (position % GRID_C * TILE_COLS).astype(jnp.int32)
            zero = jnp.zeros((), jnp.int32)
            sizes = (TILE_ROWS + 2 * R_MAX, TILE_COLS + 2 * R_MAX, dim)
            key_tile = lax.dynamic_slice(pad_keys, (row_start, col_start, zero), sizes)
            value_tile = lax.dynamic_slice(pad_values, (row_start, col_start, zero), sizes)
            query_tile = frame_queries[tile_idx]
            return neighborhood(query_tile, key_tile, value_tile, radii, row_start, col_start, HEIGHT, WIDTH)
        local_list.append(lax.map(one_tile, jnp.arange(TILES, dtype=jnp.int32)))
        key_rows = keys[frame].reshape(-1, head_count, head_dim)
        value_rows = values[frame].reshape(-1, head_count, head_dim)
        feature = jax.nn.relu(key_rows)
        state = state + jnp.einsum('khd,khe->hde', feature, value_rows, precision=lax.Precision.HIGHEST)
        zsum = zsum + lax.optimization_barrier(jnp.sum(feature, axis=0))
        vsum = vsum + lax.optimization_barrier(jnp.sum(value_rows, axis=0))
        count = jnp.float32((frame + 1) * HEIGHT * WIDTH)
        query_rows = queries[frame].reshape(-1, head_count, head_dim)
        global_list.append(linear_out(query_rows, state, zsum, vsum, count).reshape(queries.shape[1:]))
    return (jnp.stack(local_list), jnp.stack(global_list))
```

```python
import functools
import math

import jax
import jax.numpy as jnp
from jax import lax
from jax.experimental import pallas as pl
from jax.experimental.pallas import tpu as pltpu
from jax.sharding import PartitionSpec as P

R_MAX = 4
FAR = 1e6
EXCLUDED = -1e30
MESH = pl.DeviceIdType.MESH


def split(x):
    high = x.astype(jnp.bfloat16)
    low = (x - high.astype(jnp.float32)).astype(jnp.bfloat16)
    return high, low


def dot3(a, b, over):
    def one(x, y):
        return lax.dot_general(x, y, (over, ((), ())), preferred_element_type=jnp.float32)

    return one(a[0], b[0]) + (one(a[0], b[1]) + one(a[1], b[0]))


def pick(side, after, before):
    if isinstance(side, int):
        return after if side > 0 else before
    return jnp.where(side > 0, after, before)


def guarded(when, act):
    if when is True:
        act()
    else:
        pl.when(when)(act)


def sides_of(count, here):
    if count == 1:
        return []
    if count == 2:
        return [(1 - 2 * here, True, 0)]
    return [(-1, here > 0, 1), (1, here < count - 1, 0)]


def strip_plan(rows, cols, grid_rows, grid_cols, grid_row, grid_col):
    down, across = sides_of(grid_rows, grid_row), sides_of(grid_cols, grid_col)
    raw, place, offset = [], {}, 0
    kinds = (
        [(None, j) for j in range(len(across))]
        + [(i, None) for i in range(len(down))]
        + [(i, j) for i in range(len(down)) for j in range(len(across))]
    )
    for i, j in kinds:
        tokens = (rows if i is None else R_MAX) * (cols if j is None else R_MAX)
        place[(i, j)] = offset
        raw.append((i, j, offset, tokens))
        offset += tokens
    strips = []
    for i, j, start, tokens in raw:
        dn = (0, True, None) if i is None else down[i]
        ac = (0, True, None) if j is None else across[j]
        if dn[1] is True:
            there = ac[1]
        elif ac[1] is True:
            there = dn[1]
        else:
            there = jnp.logical_and(dn[1], ac[1])
        opposite = place[(None if i is None else dn[2], None if j is None else ac[2])]
        strips.append((None if i is None else dn[0], None if j is None else ac[0], there, start, tokens, opposite))
    return strips, offset


def kernel(sizes, radii, q, k, v, local, glob, halo, send, near, far, acc, top, total, state, full,
           first, chain, passed, others, halo_send, halo_recv, step_send, step_recv, cross_send, cross_recv):
    frames, tiles, grid_rows, grid_cols, rows, cols, heads, width = sizes
    tokens = rows * cols
    half = heads // 2
    frame, tile = lax.axis_index("block"), lax.axis_index("tile")
    position = lax.rem(tile + 1, tiles)
    grid_row, grid_col = position // grid_cols, lax.rem(position, grid_cols)
    strips, used = strip_plan(rows, cols, grid_rows, grid_cols, grid_row, grid_col)
    padded = halo.shape[2]
    parity, couple = lax.rem(tile, 2), tile // 2
    peer = tile + 1 - 2 * parity
    couples = tiles // 2
    scale = 1.0 / math.sqrt(width)

    def neighbor(strip):
        r = grid_row + (0 if strip[0] is None else strip[0])
        c = grid_col + (0 if strip[1] is None else strip[1])
        return lax.rem(r * grid_cols + c + tiles - 1, tiles)

    def alike(d):
        return lax.rem(couple + d, couples) * 2 + parity

    if grid_rows == 2 and grid_cols == 2:
        if padded > used:
            halo[:, :, pl.ds(used, padded - used), :] = jnp.zeros((heads, 2, padded - used, width), jnp.float32)
    else:
        halo[...] = jnp.zeros_like(halo)

    barrier = pltpu.get_barrier_semaphore()

    def greet(axis, device):
        pl.semaphore_signal(barrier, inc=1, device_id={axis: device}, device_id_type=MESH)

    meetings = [(strip[2], "tile", neighbor(strip)) for strip in strips]
    if not (grid_rows == 2 and grid_cols == 2):
        meetings += [(True, "tile", peer)] + [(True, "tile", alike(d)) for d in range(1, couples)]
    meetings += [(frame > 0, "block", frame - 1), (frame < frames - 1, "block", frame + 1)]
    for there, axis, device in meetings:
        guarded(there, functools.partial(greet, axis, device))

    for part, x in enumerate((k, v)):
        for down, across, there, start, count, _ in strips:
            if down is None:
                for r in range(rows):
                    strip = pick(across, x[r * cols + cols - R_MAX:(r + 1) * cols, :], x[r * cols:r * cols + R_MAX, :])
                    for h in range(heads):
                        send[h, part, start + r * R_MAX:start + (r + 1) * R_MAX, :] = strip[:, h * width:(h + 1) * width]
                continue
            begin = pick(down, tokens - R_MAX * cols, 0)
            begin = begin if isinstance(begin, int) else pl.multiple_of(begin, cols)
            block = x[pl.ds(begin, R_MAX * cols), :]
            if across is None:
                for h in range(heads):
                    send[h, part, start:start + count, :] = block[:, h * width:(h + 1) * width]
                continue
            for r in range(R_MAX):
                row = block[r * cols:(r + 1) * cols]
                strip = pick(across, row[cols - R_MAX:], row[:R_MAX])
                for h in range(heads):
                    send[h, part, start + r * R_MAX:start + (r + 1) * R_MAX, :] = strip[:, h * width:(h + 1) * width]

    present = sum(1 if there is True else jnp.where(there, 1, 0) for there, _, _ in meetings)
    pl.semaphore_wait(barrier, present)

    def halo_copy(place, h):
        strip = strips[place]
        return pltpu.make_async_remote_copy(
            src_ref=send.at[h, :, pl.ds(strip[3], strip[4]), :],
            dst_ref=halo.at[h, :, pl.ds(strip[5], strip[4]), :],
            send_sem=halo_send.at[place, h],
            recv_sem=halo_recv.at[place, h],
            device_id={"tile": neighbor(strip)},
            device_id_type=MESH,
        )

    def halo_arrival(place, h):
        strip = strips[place]
        return pltpu.make_async_remote_copy(
            src_ref=send.at[h, :, pl.ds(strip[3], strip[4]), :],
            dst_ref=halo.at[h, :, pl.ds(strip[3], strip[4]), :],
            send_sem=halo_send.at[place, h],
            recv_sem=halo_recv.at[opposite_place[place], h],
            device_id={"tile": neighbor(strip)},
            device_id_type=MESH,
        )

    opposite_place = [[s[3] for s in strips].index(strip[5]) for strip in strips]

    def send_halo(h):
        for place, strip in enumerate(strips):
            guarded(strip[2], lambda place=place: halo_copy(place, h).start())

    def await_halo(h):
        for place, strip in enumerate(strips):
            guarded(strip[2], lambda place=place: halo_arrival(place, h).wait_recv())

    def lanes(h):
        return pl.ds(pl.multiple_of(h * width, width), width)

    def to_peer():
        return pltpu.make_async_remote_copy(
            src_ref=state.at[pl.ds((1 - parity) * half, half)], dst_ref=first,
            send_sem=step_send.at[0], recv_sem=step_recv.at[0],
            device_id={"tile": peer}, device_id_type=MESH)

    def to_next():
        return pltpu.make_async_remote_copy(
            src_ref=passed, dst_ref=chain,
            send_sem=step_send.at[1], recv_sem=step_recv.at[1],
            device_id={"block": frame + 1}, device_id_type=MESH)

    def to_alike(d):
        return pltpu.make_async_remote_copy(
            src_ref=passed, dst_ref=others.at[d - 1],
            send_sem=cross_send.at[d - 1], recv_sem=cross_recv.at[d - 1],
            device_id={"tile": alike(d)}, device_id_type=MESH)

    def hand_back():
        return pltpu.make_async_remote_copy(
            src_ref=full.at[pl.ds(parity * half, half)], dst_ref=full.at[pl.ds(parity * half, half)],
            send_sem=step_send.at[2], recv_sem=step_recv.at[2],
            device_id={"tile": peer}, device_id_type=MESH)

    send_halo(0)

    def one_state(h, _):
        feature = jnp.maximum(k[:, lanes(h)], 0.0)
        value = v[:, lanes(h)]
        state[h, 0:width, :] = dot3(split(feature), split(value), ((0,), (0,)))
        line = lax.broadcasted_iota(jnp.int32, (8, width), 0)
        zsum = jnp.sum(feature, axis=0, keepdims=True)
        vsum = jnp.sum(value, axis=0, keepdims=True)
        state[h, width:width + 8, :] = jnp.where(line == 0, zsum, jnp.where(line == 1, vsum, 0.0))
        return 0

    lax.fori_loop(0, heads, one_state, 0)
    to_peer().start()
    send_halo(1)

    def over(count_, axis, shape, per):
        index = lax.broadcasted_iota(jnp.int32, shape, axis).astype(jnp.float32)
        major = jnp.floor((index + 0.5) * (1.0 / per))
        return index, major, index - major * per

    _, q_row, q_col = over(tokens, 0, (tokens, 1), cols)
    _, k_row, k_col = over(tokens, 1, (1, tokens), cols)
    near[...] = jnp.maximum(jnp.abs(q_row - k_row), jnp.abs(q_col - k_col))
    index = lax.broadcasted_iota(jnp.int32, (1, padded), 1).astype(jnp.float32)
    h_row, h_col = jnp.full((1, padded), FAR, jnp.float32), jnp.full((1, padded), FAR, jnp.float32)
    for down, across, there, start, count, _ in strips:
        per = cols if across is None else R_MAX
        own = index - float(start)
        major = jnp.floor((own + 0.5) * (1.0 / per))
        minor = own - major * per
        row = major if down is None else major + pick(down, float(rows), float(-R_MAX))
        col = minor if across is None else minor + pick(across, float(cols), float(-R_MAX))
        if there is not True:
            row = row + jnp.where(there, 0.0, FAR)
        inside = jnp.logical_and(index >= float(start), index < float(start + count))
        h_row, h_col = jnp.where(inside, row, h_row), jnp.where(inside, col, h_col)
    far[...] = jnp.maximum(jnp.abs(q_row - h_row), jnp.abs(q_col - h_col))

    def own_part(h, _):
        radius = radii[h].astype(jnp.float32)
        score = dot3(split(q[:, lanes(h)]), split(k[:, lanes(h)]), ((1,), (1,))) * scale
        score = jnp.where(near[...] <= radius, score, EXCLUDED)
        highest = jnp.max(score, axis=1, keepdims=True)
        weight = jnp.exp(score - highest)
        top[h] = highest
        total[h] = jnp.sum(weight, axis=1, keepdims=True)
        acc[h] = dot3(split(weight), split(v[:, lanes(h)]), ((1,), (0,)))
        return 0

    lax.fori_loop(0, heads, own_part, 0)

    to_peer().wait_recv()
    passed[...] = state[pl.ds(parity * half, half)] + first[...]

    def receive():
        to_next().wait_recv()
        passed[...] = passed[...] + chain[...]

    pl.when(frame > 0)(receive)
    pl.when(frame < frames - 1)(lambda: to_next().start())
    for d in range(1, couples):
        to_alike(d).start()
    for h in range(2, heads):
        send_halo(h)

    def outer_part(h):
        await_halo(h)
        radius = radii[h].astype(jnp.float32)
        score = dot3(split(q[:, lanes(h)]), split(halo[h, 0]), ((1,), (1,))) * scale
        score = jnp.where(far[...] <= radius, score, EXCLUDED)
        highest = jnp.maximum(top[h], jnp.max(score, axis=1, keepdims=True))
        weight = jnp.exp(score - highest)
        fade = jnp.exp(top[h] - highest)
        below = total[h] * fade + jnp.sum(weight, axis=1, keepdims=True)
        above = acc[h] * fade + dot3(split(weight), split(halo[h, 1]), ((1,), (0,)))
        local[:, lanes(h)] = above / below

    def outer_step(h, _):
        outer_part(h)
        return 0

    lax.fori_loop(0, 2, outer_step, 0)

    mine = passed[...]
    for d in range(1, couples):
        to_alike(d).wait_recv()
        mine = mine + others[d - 1]
    full[pl.ds(parity * half, half)] = mine
    hand_back().start()

    pltpu.make_async_remote_copy(
        src_ref=full.at[pl.ds((1 - parity) * half, half)], dst_ref=full.at[pl.ds((1 - parity) * half, half)],
        send_sem=step_send.at[2], recv_sem=step_recv.at[2],
        device_id={"tile": peer}, device_id_type=MESH).wait_recv()

    seen = ((frame + 1) * (tiles * tokens)).astype(jnp.float32)

    def global_part(h, _):
        feature = jnp.maximum(q[:, lanes(h)], 0.0)
        numer = dot3(split(feature), split(full[h, 0:width, :]), ((1,), (0,))) * scale + full[h, width + 1:width + 2, :]
        denom = jnp.sum(feature * full[h, width:width + 1, :], axis=1, keepdims=True) * scale + seen
        glob[:, lanes(h)] = numer / denom
        return 0

    lax.fori_loop(0, heads, global_part, 0)
    lax.fori_loop(2, heads, outer_step, 0)

    for h in range(heads):
        for place, strip in enumerate(strips):
            guarded(strip[2], lambda place=place, h=h: halo_copy(place, h).wait_send())
    to_peer().wait_send()
    pl.when(frame < frames - 1)(lambda: to_next().wait_send())
    for d in range(1, couples):
        to_alike(d).wait_send()
    hand_back().wait_send()


def solution(mesh):
    frames, tiles = mesh.shape["block"], mesh.shape["tile"]
    grid_cols = min(4, tiles // 2)
    grid_rows = tiles // grid_cols

    def body(queries, keys, values, radii):
        rows, cols, dim = queries.shape[2:]
        heads = radii.shape[0]
        width = dim // heads
        tokens = rows * cols
        strips, used = strip_plan(rows, cols, grid_rows, grid_cols, 0, 0)
        padded = -(-used // 128) * 128
        half, depth, couples = heads // 2, width + 8, tiles // 2
        flat = [x.reshape(tokens, dim) for x in (queries, keys, values)]
        f32 = jnp.float32
        vmem = pl.BlockSpec(memory_space=pltpu.VMEM)
        local, glob = pl.pallas_call(
            functools.partial(kernel, (frames, tiles, grid_rows, grid_cols, rows, cols, heads, width)),
            out_shape=[jax.ShapeDtypeStruct((tokens, dim), f32)] * 2,
            in_specs=[pl.BlockSpec(memory_space=pltpu.SMEM), vmem, vmem, vmem],
            out_specs=[vmem, vmem],
            scratch_shapes=[
                pltpu.VMEM((heads, 2, padded, width), f32),
                pltpu.VMEM((heads, 2, padded, width), f32),
                pltpu.VMEM((tokens, tokens), f32),
                pltpu.VMEM((tokens, padded), f32),
                pltpu.VMEM((heads, tokens, width), f32),
                pltpu.VMEM((heads, tokens, 1), f32),
                pltpu.VMEM((heads, tokens, 1), f32),
                pltpu.VMEM((heads, depth, width), f32),
                pltpu.VMEM((heads, depth, width), f32),
                pltpu.VMEM((half, depth, width), f32),
                pltpu.VMEM((half, depth, width), f32),
                pltpu.VMEM((half, depth, width), f32),
                pltpu.VMEM((max(couples - 1, 1), half, depth, width), f32),
                pltpu.SemaphoreType.DMA((len(strips), heads)),
                pltpu.SemaphoreType.DMA((len(strips), heads)),
                pltpu.SemaphoreType.DMA((3,)),
                pltpu.SemaphoreType.DMA((3,)),
                pltpu.SemaphoreType.DMA((max(couples - 1, 1),)),
                pltpu.SemaphoreType.DMA((max(couples - 1, 1),)),
            ],
            compiler_params=pltpu.CompilerParams(
                collective_id=0, has_side_effects=True, vmem_limit_bytes=56 * 1024 * 1024
            ),
            cost_estimate=pl.CostEstimate(
                flops=2 * 3 * tokens * dim * 2 * (tokens + padded + width),
                bytes_accessed=5 * tokens * dim * 4,
                transcendentals=tokens * (tokens + padded) * heads,
            ),
        )(radii, *flat)
        return local.reshape(queries.shape), glob.reshape(queries.shape)

    spec = P(("groups", "block"), "tile", None, None, None)
    return jax.shard_map(
        body,
        mesh=mesh,
        in_specs=(spec, spec, spec, P()),
        out_specs=(spec, spec),
        check_vma=False,
    )
```

```python
import functools
import math

import jax
import jax.numpy as jnp
from jax import lax
from jax.experimental import pallas as pl
from jax.experimental.pallas import tpu as pltpu
from jax.sharding import PartitionSpec as P

R_MAX = 4
FAR = 1e6
EXCLUDED = -1e30
MESH = pl.DeviceIdType.MESH


def split(x):
    high = x.astype(jnp.bfloat16)
    low = (x - high.astype(jnp.float32)).astype(jnp.bfloat16)
    return high, low


def dot3(a, b, over):
    def one(x, y):
        return lax.dot_general(x, y, (over, ((), ())), preferred_element_type=jnp.float32)

    return one(a[0], b[0]) + (one(a[0], b[1]) + one(a[1], b[0]))


def pick(side, after, before):
    if isinstance(side, int):
        return after if side > 0 else before
    return jnp.where(side > 0, after, before)


def guarded(when, act):
    if when is True:
        act()
    else:
        pl.when(when)(act)


def sides_of(count, here):
    if count == 1:
        return []
    if count == 2:
        return [(1 - 2 * here, True, 0)]
    return [(-1, here > 0, 1), (1, here < count - 1, 0)]


def strip_plan(reach, rows, cols, grid_rows, grid_cols, grid_row, grid_col):
    down, across = sides_of(grid_rows, grid_row), sides_of(grid_cols, grid_col)
    raw, place, offset = [], {}, 0
    kinds = (
        [(None, j) for j in range(len(across))]
        + [(i, None) for i in range(len(down))]
        + [(i, j) for i in range(len(down)) for j in range(len(across))]
    )
    for i, j in kinds:
        tokens = R_MAX * R_MAX
        if i is None:
            tokens = rows * reach
        elif j is None:
            tokens = reach * cols
        place[(i, j)] = offset
        raw.append((i, j, offset, tokens))
        offset += tokens
    strips = []
    for i, j, start, tokens in raw:
        dn = (0, True, None) if i is None else down[i]
        ac = (0, True, None) if j is None else across[j]
        if dn[1] is True:
            there = ac[1]
        elif ac[1] is True:
            there = dn[1]
        else:
            there = jnp.logical_and(dn[1], ac[1])
        opposite = place[(None if i is None else dn[2], None if j is None else ac[2])]
        strips.append((None if i is None else dn[0], None if j is None else ac[0], there, start, tokens, opposite))
    return strips, offset


def padded_to(used):
    return -(-used // 128) * 128


def kernel(sizes, widths, radii, q, k, v, local, glob, radius, q_slot, k_slot, v_slot, halo, send, near, far, acc, top, total, state,
           full, first, chain, passed, others, halo_send, halo_recv, step_send, step_recv, cross_send, cross_recv):
    frames, tiles, grid_rows, grid_cols, rows, cols, heads, width = sizes
    tokens = rows * cols
    half = heads // 2
    frame, tile = lax.axis_index("block"), lax.axis_index("tile")
    position = lax.rem(tile + 1, tiles)
    grid_row, grid_col = position // grid_cols, lax.rem(position, grid_cols)
    kinds = sorted(set(widths))
    plans = {w: strip_plan(w, rows, cols, grid_rows, grid_cols, grid_row, grid_col) for w in kinds}
    strips_of = [plans[w][0] for w in widths]
    strips = strips_of[0]
    fold = grid_rows == 2 and grid_cols == 2
    parity, couple = lax.rem(tile, 2), tile // 2
    peer = tile + 1 - 2 * parity
    couples = tiles // 2
    scale = 1.0 / math.sqrt(width)

    def neighbor(strip):
        r = grid_row + (0 if strip[0] is None else strip[0])
        c = grid_col + (0 if strip[1] is None else strip[1])
        return lax.rem(r * grid_cols + c + tiles - 1, tiles)

    def alike(d):
        return lax.rem(couple + d, couples) * 2 + parity

    for h, w in enumerate(widths):
        used = plans[w][1]
        empty = used if fold else 0
        if padded_to(used) > empty:
            halo[h, :, pl.ds(empty, padded_to(used) - empty), :] = jnp.zeros(
                (2, padded_to(used) - empty, width), jnp.float32)

    barrier = pltpu.get_barrier_semaphore()

    def greet(axis, device):
        pl.semaphore_signal(barrier, inc=1, device_id={axis: device}, device_id_type=MESH)

    meetings = [(strip[2], "tile", neighbor(strip)) for strip in strips]
    if not fold:
        meetings += [(True, "tile", peer)] + [(True, "tile", alike(d)) for d in range(1, couples)]
    meetings += [(frame > 0, "block", frame - 1), (frame < frames - 1, "block", frame + 1)]
    for there, axis, device in meetings:
        guarded(there, functools.partial(greet, axis, device))

    radius_of = [radii[h] for h in range(heads)]
    slot_of = []
    for h in range(heads):
        slot_of.append(sum(
            jnp.where(radius_of[g] >= radius_of[h] if g < h else radius_of[g] > radius_of[h], 1, 0)
            for g in range(heads) if g != h))
    for j in range(heads):
        radius[j] = sum(jnp.where(slot_of[h] == j, radius_of[h], 0) for h in range(heads))

    def lanes(h):
        return pl.ds(pl.multiple_of(h * width, width), width)

    def chosen(j, part_of):
        value = part_of(0)
        for h in range(1, heads):
            value = jnp.where(slot_of[h] == j, part_of(h), value)
        return value

    def pack(j):
        w = widths[j]
        for part, x in enumerate((k, v)):
            def taken(rows_of, x=x):
                return chosen(j, lambda h: x[rows_of, h * width:(h + 1) * width])

            for down, across, there, start, count, _ in strips_of[j]:
                if down is None:
                    for r in range(rows):
                        after, before = slice(r * cols + cols - w, (r + 1) * cols), slice(r * cols, r * cols + w)
                        strip = chosen(j, lambda h: pick(
                            across, x[after, h * width:(h + 1) * width], x[before, h * width:(h + 1) * width]))
                        send[j, part, start + r * w:start + (r + 1) * w, :] = strip
                    continue
                deep = w if across is None else R_MAX
                begin = pick(down, tokens - deep * cols, 0)
                begin = begin if isinstance(begin, int) else pl.multiple_of(begin, 8)
                block = taken(pl.ds(begin, deep * cols))
                if across is None:
                    send[j, part, start:start + count, :] = block
                    continue
                for r in range(R_MAX):
                    row = block[r * cols:(r + 1) * cols]
                    strip = pick(across, row[cols - R_MAX:], row[:R_MAX])
                    send[j, part, start + r * R_MAX:start + (r + 1) * R_MAX, :] = strip

    def one_state(h, _):
        feature = jnp.maximum(k[:, lanes(h)], 0.0)
        value = v[:, lanes(h)]
        state[h, 0:width, :] = dot3(split(feature), split(value), ((0,), (0,)))
        line = lax.broadcasted_iota(jnp.int32, (8, width), 0)
        zsum = jnp.sum(feature, axis=0, keepdims=True)
        vsum = jnp.sum(value, axis=0, keepdims=True)
        state[h, width:width + 8, :] = jnp.where(line == 0, zsum, jnp.where(line == 1, vsum, 0.0))
        return 0

    lax.fori_loop(0, heads, one_state, 0)
    present = sum(1 if there is True else jnp.where(there, 1, 0) for there, _, _ in meetings)
    pl.semaphore_wait(barrier, present)


    def halo_copy(place, h):
        strip = strips_of[h][place]
        return pltpu.make_async_remote_copy(
            src_ref=send.at[h, :, pl.ds(strip[3], strip[4]), :],
            dst_ref=halo.at[h, :, pl.ds(strip[5], strip[4]), :],
            send_sem=halo_send.at[place, h],
            recv_sem=halo_recv.at[place, h],
            device_id={"tile": neighbor(strip)},
            device_id_type=MESH,
        )

    def halo_arrival(place, h):
        strip = strips_of[h][place]
        return pltpu.make_async_remote_copy(
            src_ref=send.at[h, :, pl.ds(strip[3], strip[4]), :],
            dst_ref=halo.at[h, :, pl.ds(strip[3], strip[4]), :],
            send_sem=halo_send.at[place, h],
            recv_sem=halo_recv.at[opposite_place[place], h],
            device_id={"tile": neighbor(strip)},
            device_id_type=MESH,
        )

    opposite_place = [[s[3] for s in strips].index(strip[5]) for strip in strips]

    def send_halo(h):
        for place, strip in enumerate(strips):
            guarded(strip[2], lambda place=place: halo_copy(place, h).start())

    def await_halo(h):
        for place, strip in enumerate(strips):
            guarded(strip[2], lambda place=place: halo_arrival(place, h).wait_recv())

    def remote(src, dst, stage, p, device):
        return pltpu.make_async_remote_copy(
            src_ref=src, dst_ref=dst, send_sem=step_send.at[stage, p], recv_sem=step_recv.at[stage, p],
            device_id=device, device_id_type=MESH)

    def to_peer(p):
        return remote(state.at[(1 - parity) * half + p], first.at[p], 0, p, {"tile": peer})

    def to_next(p):
        return remote(passed.at[p], chain.at[p], 1, p, {"block": frame + 1})

    def to_alike(d, p):
        return pltpu.make_async_remote_copy(
            src_ref=passed.at[p], dst_ref=others.at[d - 1, p],
            send_sem=cross_send.at[d - 1, p], recv_sem=cross_recv.at[d - 1, p],
            device_id={"tile": alike(d)}, device_id_type=MESH)

    def hand_back(p):
        return remote(full.at[parity * half + p], full.at[parity * half + p], 2, p, {"tile": peer})

    def handed_back(p):
        return remote(full.at[(1 - parity) * half + p], full.at[(1 - parity) * half + p], 2, p, {"tile": peer})

    early = next(n for n in range(1, heads + 1) if n == heads or sum(widths[:n]) >= 2 * R_MAX)
    late = heads if early >= heads - 1 else heads - 1
    for p in range(half):
        to_peer(p).start()
    for j in range(early):
        pack(j)
        send_halo(j)

    def receive(p):
        to_next(p).wait_recv()
        passed[p] = passed[p] + chain[p]

    for p in range(half):
        to_peer(p).wait_recv()
        passed[p] = state[parity * half + p] + first[p]
        pl.when(frame > 0)(functools.partial(receive, p))
        pl.when(frame < frames - 1)(lambda p=p: to_next(p).start())
        for d in range(1, couples):
            to_alike(d, p).start()
    for j in range(early, late):
        pack(j)
        send_halo(j)
    for j in range(late, heads):
        pack(j)

    def over(count_, axis, shape, per):
        index = lax.broadcasted_iota(jnp.int32, shape, axis).astype(jnp.float32)
        major = jnp.floor((index + 0.5) * (1.0 / per))
        return index, major, index - major * per

    _, q_row, q_col = over(tokens, 0, (tokens, 1), cols)
    _, k_row, k_col = over(tokens, 1, (1, tokens), cols)
    near[...] = jnp.maximum(jnp.abs(q_row - k_row), jnp.abs(q_col - k_col))
    for kind, w in enumerate(kinds):
        padded = padded_to(plans[w][1])
        index = lax.broadcasted_iota(jnp.int32, (1, padded), 1).astype(jnp.float32)
        h_row, h_col = jnp.full((1, padded), FAR, jnp.float32), jnp.full((1, padded), FAR, jnp.float32)
        for down, across, there, start, count, _ in plans[w][0]:
            deep = R_MAX if down is not None and across is not None else w
            per = cols if across is None else deep
            own = index - float(start)
            major = jnp.floor((own + 0.5) * (1.0 / per))
            minor = own - major * per
            row = major if down is None else major + pick(down, float(rows), float(-deep))
            col = minor if across is None else minor + pick(across, float(cols), float(-deep))
            if there is not True:
                row = row + jnp.where(there, 0.0, FAR)
            inside = jnp.logical_and(index >= float(start), index < float(start + count))
            h_row, h_col = jnp.where(inside, row, h_row), jnp.where(inside, col, h_col)
        far[kind, :, 0:padded] = jnp.maximum(jnp.abs(q_row - h_row), jnp.abs(q_col - h_col))

    for j in range(heads):
        for x, x_slot in ((q, q_slot), (k, k_slot), (v, v_slot)):
            x_slot[j] = chosen(j, lambda h: x[:, h * width:(h + 1) * width])

    def own_part(j, _):
        reach = radius[j].astype(jnp.float32)
        score = dot3(split(q_slot[j]), split(k_slot[j]), ((1,), (1,))) * scale
        score = jnp.where(near[...] <= reach, score, EXCLUDED)
        highest = jnp.max(score, axis=1, keepdims=True)
        weight = jnp.exp(score - highest)
        top[j] = highest
        total[j] = jnp.sum(weight, axis=1, keepdims=True)
        acc[j] = dot3(split(weight), split(v_slot[j]), ((1,), (0,)))
        return 0

    lax.fori_loop(0, heads, own_part, 0)

    def outer_part(j):
        await_halo(j)
        size, kind = padded_to(plans[widths[j]][1]), kinds.index(widths[j])
        reach = radius[j].astype(jnp.float32)
        score = dot3(split(q_slot[j]), split(halo[j, 0, 0:size]), ((1,), (1,))) * scale
        score = jnp.where(far[kind, :, 0:size] <= reach, score, EXCLUDED)
        highest = jnp.maximum(top[j], jnp.max(score, axis=1, keepdims=True))
        weight = jnp.exp(score - highest)
        fade = jnp.exp(top[j] - highest)
        below = total[j] * fade + jnp.sum(weight, axis=1, keepdims=True)
        above = acc[j] * fade + dot3(split(weight), split(halo[j, 1, 0:size]), ((1,), (0,)))
        acc[j] = above / below

    for p in range(half):
        mine = passed[p]
        for d in range(1, couples):
            to_alike(d, p).wait_recv()
            mine = mine + others[d - 1, p]
        full[parity * half + p] = mine
        hand_back(p).start()
    for j in range(late, heads):
        send_halo(j)
    for j in range(early):
        outer_part(j)

    seen = ((frame + 1) * (tiles * tokens)).astype(jnp.float32)

    def global_part(h):
        feature = jnp.maximum(q[:, lanes(h)], 0.0)
        numer = dot3(split(feature), split(full[h, 0:width, :]), ((1,), (0,))) * scale + full[h, width + 1:width + 2, :]
        denom = jnp.sum(feature * full[h, width:width + 1, :], axis=1, keepdims=True) * scale + seen
        glob[:, lanes(h)] = numer / denom

    for p in range(half):
        global_part(parity * half + p)
    for j in range(early, late):
        outer_part(j)
    for p in range(half):
        handed_back(p).wait_recv()
        global_part((1 - parity) * half + p)
    for j in range(late, heads):
        outer_part(j)
    for h in range(heads):
        value = acc[0]
        for j in range(1, heads):
            value = jnp.where(slot_of[h] == j, acc[j], value)
        local[:, h * width:(h + 1) * width] = value

    for h in range(heads):
        for place, strip in enumerate(strips_of[h]):
            guarded(strip[2], lambda place=place, h=h: halo_copy(place, h).wait_send())
    for p in range(half):
        to_peer(p).wait_send()
        pl.when(frame < frames - 1)(lambda p=p: to_next(p).wait_send())
        for d in range(1, couples):
            to_alike(d, p).wait_send()
        hand_back(p).wait_send()


def solution(mesh):
    frames, tiles = mesh.shape["block"], mesh.shape["tile"]
    grid_cols = min(4, tiles // 2)
    grid_rows = tiles // grid_cols

    def body(queries, keys, values, radii):
        rows, cols, dim = queries.shape[2:]
        heads = radii.shape[0]
        width = dim // heads
        tokens = rows * cols
        strips, used = strip_plan(R_MAX, rows, cols, grid_rows, grid_cols, 0, 0)
        padded = padded_to(used)
        half, depth, couples = heads // 2, width + 8, tiles // 2
        flat = [x.reshape(tokens, dim) for x in (queries, keys, values)]
        f32 = jnp.float32
        vmem = pl.BlockSpec(memory_space=pltpu.VMEM)
        def run(widths, number, *operands):
            return pl.pallas_call(
                functools.partial(kernel, (frames, tiles, grid_rows, grid_cols, rows, cols, heads, width), widths),
                out_shape=[jax.ShapeDtypeStruct((tokens, dim), f32)] * 2,
                in_specs=[pl.BlockSpec(memory_space=pltpu.SMEM), vmem, vmem, vmem],
                out_specs=[vmem, vmem],
                scratch_shapes=[
                    pltpu.SMEM((heads,), jnp.int32),
                    pltpu.VMEM((heads, tokens, width), f32),
                    pltpu.VMEM((heads, tokens, width), f32),
                    pltpu.VMEM((heads, tokens, width), f32),
                    pltpu.VMEM((heads, 2, padded, width), f32),
                    pltpu.VMEM((heads, 2, padded, width), f32),
                    pltpu.VMEM((tokens, tokens), f32),
                    pltpu.VMEM((2, tokens, padded), f32),
                    pltpu.VMEM((heads, tokens, width), f32),
                    pltpu.VMEM((heads, tokens, 1), f32),
                    pltpu.VMEM((heads, tokens, 1), f32),
                    pltpu.VMEM((heads, depth, width), f32),
                    pltpu.VMEM((heads, depth, width), f32),
                    pltpu.VMEM((half, depth, width), f32),
                    pltpu.VMEM((half, depth, width), f32),
                    pltpu.VMEM((half, depth, width), f32),
                    pltpu.VMEM((max(couples - 1, 1), half, depth, width), f32),
                    pltpu.SemaphoreType.DMA((len(strips), heads)),
                    pltpu.SemaphoreType.DMA((len(strips), heads)),
                    pltpu.SemaphoreType.DMA((3, half)),
                    pltpu.SemaphoreType.DMA((3, half)),
                    pltpu.SemaphoreType.DMA((max(couples - 1, 1), half)),
                    pltpu.SemaphoreType.DMA((max(couples - 1, 1), half)),
                ],
                compiler_params=pltpu.CompilerParams(
                    collective_id=number, has_side_effects=True, vmem_limit_bytes=56 * 1024 * 1024
                ),
                cost_estimate=pl.CostEstimate(
                    flops=2 * 3 * tokens * dim * 2 * (tokens + padded + width),
                    bytes_accessed=5 * tokens * dim * 4,
                    transcendentals=tokens * (tokens + padded) * heads,
                ),
            )(*operands)

        narrow = R_MAX // 2
        variants = [
            functools.partial(run, (R_MAX,) * wide + (narrow,) * (heads - wide), wide - 1)
            for wide in range(1, heads + 1)
        ]
        local, glob = lax.switch(jnp.sum(radii > narrow) - 1, variants, radii, *flat)
        return local.reshape(queries.shape), glob.reshape(queries.shape)

    spec = P(("groups", "block"), "tile", None, None, None)
    return jax.shard_map(
        body,
        mesh=mesh,
        in_specs=(spec, spec, spec, P()),
        out_specs=(spec, spec),
        check_vma=False,
    )
```
